256 devices in a mesh: dp: 64 (over x, y, z_lo, core), fsdp: 4 (over z_hi).
Axes of the slice: x: 4, y: 4, z: 8 (z_hi: 4, z_lo: 2; z = z_hi * 2 + z_lo), core: 2. Of those that a mesh axis runs over, the one named last changes fastest.
Arguments:
- step_index: int32 [1], replicated, may hold values from 0 to 999
- token_codes: int32 [64, 1024], P('dp', 'fsdp'), may hold values from 0 to 65535
- params: bfloat16 [64, 2560, 2560], P('dp', 'fsdp'), may hold values from -0.125 to 0.125
- moments: bfloat16 [64, 2560, 2560], P('dp', 'fsdp'), may hold values from -6 to 6
- second: float32 [64, 2560], P('dp', 'fsdp'), may hold values from 0.5 to 50
Outputs:
- new_params: bfloat16 [64, 2560, 2560], P('dp', 'fsdp')
- new_moments: bfloat16 [64, 2560, 2560], P('dp', 'fsdp')
- new_second: float32 [64, 2560], P('dp', 'fsdp')
The draws below stay inside these ranges and needn't reach their ends.
All inputs are finite; a program needn't handle non-finite values.
Results may differ from the reference program's by a relative error of at most 0.012.
Values may be sent and summed in bfloat16 or wider, within the bound.
No kernel may reach another device: no remote copies, remote signals or barrier semaphores. Data moves between devices by JAX's collectives and lax.ppermute only.
A program may use at most 128 MiB of HBM per device.

```python
import math
import jax
import jax.numpy as jnp
from jax import lax

WIDTH = 2560
TOK_DEV = 256
REPLICAS = 64
ROWS = 1024


def place_ends(entries, own_key, least, high):
    longest = entries.shape.index(max(entries.shape))
    spots = []
    for shift in (0, 1):
        where = [jax.random.randint(jax.random.fold_in(own_key, axis), (), 0, length) for axis, length in enumerate(entries.shape)]
        where[longest] = (where[longest] + shift) % entries.shape[longest]
        spots.append(tuple(where))
    return entries.at[spots[0]].set(least).at[spots[1]].set(high)


def steps_of(stream_key, dims, pieces, smallest, high):
    loudness = 1.0
    for dim, blocks in pieces:
        draws = jax.random.uniform(jax.random.fold_in(jax.random.fold_in(stream_key, 6), dim), (blocks,), jnp.float32, smallest / len(pieces), high / len(pieces))
        loudness = loudness * jnp.repeat(jnp.exp(draws), dims[dim] // blocks).reshape((-1,) + (1,) * (len(dims) - 1 - dim))
    return loudness


def scatter_about(stream_key, shape, deviation, bound, shards=(), kind=jnp.bfloat16):
    array = jax.random.normal(stream_key, shape, jnp.float32) * deviation
    if len(shards) > 0:
        array = steps_of(stream_key, shape, shards, -0.22, 0.18) * array
    return jnp.clip(array, min=-bound, max=bound).astype(kind)


def setup_inputs(seed: int = 0) -> dict:
    splits = jax.random.split(jax.random.key(seed), 6)
    return {
        "step_index": jax.random.randint(splits[0], (1,), 0, 1000).astype(jnp.int32),
        "token_codes": place_ends(jax.random.randint(splits[1], (REPLICAS, ROWS), 0, 65536), jax.random.fold_in(splits[1], 1), 0, 65535).astype(jnp.int32),
        "params": scatter_about(splits[2], (REPLICAS, WIDTH, WIDTH), WIDTH ** -0.5, 0.125, ((0, 64), (1, 4))),
        "moments": scatter_about(splits[3], (REPLICAS, WIDTH, WIDTH), 1.0, 6.0, ((0, 64), (1, 4))),
        "second": jnp.clip(jnp.exp(math.log(50.0) - 4.6051702 * jax.random.uniform(splits[4], (REPLICAS, WIDTH), jnp.float32) ** steps_of(splits[4], (REPLICAS, WIDTH), ((0, 64), (1, 4)), -0.2, 0.2)), 0.5, 50.0),
    }


GELU_SCALE = math.sqrt(2.0 / math.pi)
GELU_CUBIC = 0.044715
BETA_ONE = 0.9
BETA_TWO = 0.999
LEARN_RATE = 0.001
EPSILON = 1e-08

def encode(code_row, width_all):
    column = jnp.arange(width_all, dtype=jnp.int32)
    turns = (code_row[:, None] * (2 * column[None, :] + 1) + 977 * column[None, :]) % 65536
    angle = turns.astype(jnp.float32) * (2.0 * math.pi / 65536.0)
    return (math.sqrt(2.0) * jnp.cos(angle)).astype(jnp.bfloat16)

def gelu_pair(hidden):
    inner = GELU_SCALE * (hidden + GELU_CUBIC * hidden * hidden * hidden)
    tangent = jnp.tanh(inner)
    value = 0.5 * hidden * (1.0 + tangent)
    slope = 0.5 * (1.0 + tangent) + 0.5 * hidden * (1.0 - tangent * tangent) * GELU_SCALE * (1.0 + 3.0 * GELU_CUBIC * hidden * hidden)
    return (value, slope)

def hidden_error(own_feats, hidden, tok_rows):
    value, slope = gelu_pair(hidden)
    blocks = own_feats.astype(jnp.float32).reshape(-1, tok_rows, own_feats.shape[1])
    following = jnp.concatenate([blocks[:, 1:], jnp.zeros_like(blocks[:, :1])], axis=1)
    keep = (jnp.arange(tok_rows) < tok_rows - 1).astype(jnp.float32)[None, :, None]
    missed = (blocks + value.reshape(blocks.shape) - following) * keep
    return (missed * slope.reshape(blocks.shape)).astype(jnp.bfloat16).reshape(hidden.shape)

def adam_mini(mixed, mom_own, mom_far, second_row, grad):
    mom_mix = 0.5 * (mom_own.astype(jnp.float32) + mom_far.astype(jnp.float32))
    mom_full = BETA_ONE * mom_mix + (1.0 - BETA_ONE) * grad
    second_new = BETA_TWO * second_row + (1.0 - BETA_TWO) * lax.optimization_barrier(jnp.mean(grad * grad, axis=-1))
    param_new = mixed.astype(jnp.float32) - LEARN_RATE * mom_full / (jnp.sqrt(second_new)[:, None] + EPSILON)
    return (param_new.astype(jnp.bfloat16), mom_full.astype(jnp.bfloat16), second_new)

def reference(step_index, token_codes, params, moments, second):
    levels = min(5, int(REPLICAS).bit_length() - 1)
    distance = jnp.left_shift(jnp.int32(1), (step_index[0] % levels).astype(jnp.int32))

    def one_replica(replica):
        partner = ((replica - distance) % REPLICAS).astype(jnp.int32)
        weights = lax.dynamic_index_in_dim(params, replica, 0, keepdims=False)
        weights_far = lax.dynamic_index_in_dim(params, partner, 0, keepdims=False)
        mom_own = lax.dynamic_index_in_dim(moments, replica, 0, keepdims=False)
        mom_far = lax.dynamic_index_in_dim(moments, partner, 0, keepdims=False)
        second_row = lax.dynamic_index_in_dim(second, replica, 0, keepdims=False)
        code_row = lax.dynamic_index_in_dim(token_codes, replica, 0, keepdims=False)
        mixed = (0.5 * (weights.astype(jnp.float32) + weights_far.astype(jnp.float32))).astype(jnp.bfloat16)
        features = encode(code_row, WIDTH)
        hidden = jnp.dot(features, mixed.T, preferred_element_type=jnp.float32)
        error = hidden_error(features, hidden, TOK_DEV)
        count = ROWS // TOK_DEV
        per_block = jnp.einsum('btj,bti->bji', error.reshape(count, TOK_DEV, WIDTH).astype(jnp.float32), features.reshape(count, TOK_DEV, WIDTH).astype(jnp.float32))
        rounded = lax.optimization_barrier(per_block.astype(jnp.bfloat16))
        grad = lax.optimization_barrier(jnp.sum(rounded.astype(jnp.float32), axis=0))
        return adam_mini(mixed, mom_own, mom_far, second_row, grad)
    new_params, new_moments, new_second = lax.map(one_replica, jnp.arange(REPLICAS, dtype=jnp.int32))
    return (new_params, new_moments, new_second)
```

```python
from functools import partial
import math

import jax
import jax.numpy as jnp
from jax import lax
from jax.experimental import pallas as pl
from jax.experimental.pallas import tpu as pltpu
from jax.sharding import PartitionSpec as P

GELU_SCALE = math.sqrt(2.0 / math.pi)
GELU_CUBIC = 0.044715
BETA_ONE = 0.9
BETA_TWO = 0.999
LEARN_RATE = 0.001
EPSILON = 1e-08
LANES = 128
BAND = 16


def turn_pair(turns):
    quarter = (turns + 8192) >> 14
    rest = (turns - (quarter << 14)).astype(jnp.float32) * (2.0 * math.pi / 65536.0)
    square = rest * rest
    sine = rest + rest * square * (
        -1.6666654611e-1 + square * (8.3321608736e-3 + square * -1.9515295891e-4)
    )
    cosine = (
        1.0
        - 0.5 * square
        + square * square * (4.166664568298827e-2 + square * (-1.388731625493765e-3 + square * 2.443315711809948e-5))
    )
    odd = (quarter & 1) == 1
    cos_size = jnp.where(odd, sine, cosine)
    sin_size = jnp.where(odd, cosine, sine)
    cos_minus = ((quarter + 1) & 2) == 2
    sin_minus = (quarter & 2) == 2
    return (jnp.where(cos_minus, -cos_size, cos_size), jnp.where(sin_minus, -sin_size, sin_size))


def features_kernel(first_ref, column_ref, row_ref, next_ref, feats_ref, change_ref):
    tokens, width_all = feats_ref.shape
    own_rows = change_ref.shape[0]
    root = math.sqrt(2.0)

    code = column_ref[...]
    step = (2 * code + 977) & 65535
    lane = lax.broadcasted_iota(jnp.int32, (tokens, LANES), 1)
    near_cos, near_sin = turn_pair((step * lane) & 65535)
    far_cos, far_sin = turn_pair((code + step * (lane * LANES)) & 65535)
    far_cos, far_sin = far_cos * root, far_sin * root
    for a in range(width_all // LANES):
        feats_ref[:, a * LANES : (a + 1) * LANES] = (
            far_cos[:, a : a + 1] * near_cos - far_sin[:, a : a + 1] * near_sin
        ).astype(feats_ref.dtype)

    blocks = own_rows // BAND

    def pieces(code):
        step = (2 * code + 977) & 65535
        band = lax.broadcasted_iota(jnp.int32, (BAND, tokens), 0)
        block = lax.broadcasted_iota(jnp.int32, (blocks, tokens), 0)
        near_cos, near_sin = turn_pair((step * band) & 65535)
        far_cos, far_sin = turn_pair((code + step * (first_ref[0] + block * BAND)) & 65535)
        return (near_cos, near_sin, far_cos * root, far_sin * root)

    def rounded(parts, a):
        near_cos, near_sin, far_cos, far_sin = parts
        value = far_cos[a : a + 1, :] * near_cos - far_sin[a : a + 1, :] * near_sin
        return value.astype(feats_ref.dtype).astype(jnp.float32)

    here, there = pieces(row_ref[0]), pieces(next_ref[0])
    for a in range(blocks):
        change_ref[a * BAND : (a + 1) * BAND, :] = rounded(here, a) - rounded(there, a)


def make_features(codes, first_col, tok_rows, own_rows, width_all):
    groups = codes.shape[0] // tok_rows
    following = jnp.roll(codes.reshape(groups, tok_rows), -1, axis=1)
    return pl.pallas_call(
        features_kernel,
        grid=(groups,),
        out_shape=(
            jax.ShapeDtypeStruct((codes.shape[0], width_all), jnp.bfloat16),
            jax.ShapeDtypeStruct((own_rows, codes.shape[0]), jnp.float32),
        ),
        in_specs=[
            pl.BlockSpec(memory_space=pltpu.SMEM),
            pl.BlockSpec((tok_rows, 1), lambda s: (s, 0)),
            pl.BlockSpec((1, 1, tok_rows), lambda s: (s, 0, 0)),
            pl.BlockSpec((1, 1, tok_rows), lambda s: (s, 0, 0)),
        ],
        out_specs=(
            pl.BlockSpec((tok_rows, width_all), lambda s: (s, 0)),
            pl.BlockSpec((own_rows, tok_rows), lambda s: (0, s)),
        ),
        compiler_params=pltpu.CompilerParams(vmem_limit_bytes=32 * 2**20),
        cost_estimate=pl.CostEstimate(
            flops=30 * codes.shape[0] * width_all, bytes_accessed=8 * 2**20, transcendentals=0
        ),
    )(
        first_col.reshape(1),
        codes.reshape(-1, 1),
        codes.reshape(groups, 1, tok_rows),
        following.reshape(groups, 1, tok_rows),
    )


def gradient_kernel(order, own_ref, far_ref, feats_ref, change_ref, mom_ref, second_ref, mixed_ref, lead_ref, *refs):
    new_ref, rate_ref = refs[::order]
    sequence = pl.program_id(0)
    own_rows, width_all = own_ref.shape
    tokens = feats_ref.shape[0]

    @pl.when(sequence == 0)
    def _():
        mixed_ref[...] = (
            0.5 * (own_ref[...].astype(jnp.float32) + far_ref[...].astype(jnp.float32))
        ).astype(mixed_ref.dtype)

    hidden = lax.dot_general(
        mixed_ref[...], feats_ref[...], (((1,), (1,)), ((), ())), preferred_element_type=jnp.float32
    )
    squared = hidden * hidden
    tangent = jnp.tanh(GELU_SCALE * hidden * (1.0 + GELU_CUBIC * squared))
    value = 0.5 * hidden * (1.0 + tangent)
    slope = 0.5 * (1.0 + tangent) + 0.5 * hidden * (1.0 - tangent * tangent) * GELU_SCALE * (
        1.0 + 3.0 * GELU_CUBIC * squared
    )
    keep = lax.broadcasted_iota(jnp.int32, (own_rows, tokens), 1) < tokens - 1
    error = jnp.where(keep, (change_ref[...] + value) * slope, 0.0).astype(jnp.bfloat16)

    tile = 256
    for low in range(0, width_all, tile):
        cut = slice(low, low + tile)
        term = lax.dot_general(
            error, feats_ref[:, cut], (((1,), (0,)), ((), ())), preferred_element_type=jnp.float32
        )
        term = term.astype(jnp.bfloat16).astype(jnp.float32)
        lead_ref[:, cut] = jnp.where(sequence == 0, term, lead_ref[:, cut] + term)

    @pl.when(sequence == pl.num_programs(0) - 1)
    def _():
        total = jnp.zeros((own_rows, 1), jnp.float32)
        for low in range(0, width_all, tile):
            cut = slice(low, low + tile)
            grad = lead_ref[:, cut]
            total += jnp.sum(grad * grad, axis=1, keepdims=True)
            lead_ref[:, cut] = (0.5 * BETA_ONE) * mom_ref[:, cut].astype(jnp.float32) + (
                1.0 - BETA_ONE
            ) * grad
        second_new = BETA_TWO * second_ref[...] + (1.0 - BETA_TWO) * (total / width_all)
        new_ref[...] = second_new
        rate_ref[...] = LEARN_RATE / (jnp.sqrt(second_new) + EPSILON)


def make_gradient(own, far, feats, change, mom_own, second_col, tok_rows, order):
    own_rows, width_all = own.shape
    groups = feats.shape[0] // tok_rows

    def whole(shape):
        return pl.BlockSpec(shape, lambda s: (0, 0), pipeline_mode=pl.Buffered(1))

    return pl.pallas_call(
        partial(gradient_kernel, order),
        grid=(groups,),
        out_shape=(
            jax.ShapeDtypeStruct(own.shape, jnp.bfloat16),
            jax.ShapeDtypeStruct(own.shape, jnp.float32),
            jax.ShapeDtypeStruct((own_rows, 1), jnp.float32),
            jax.ShapeDtypeStruct((own_rows, 1), jnp.float32),
        ),
        in_specs=[
            whole(own.shape),
            whole(own.shape),
            pl.BlockSpec((tok_rows, width_all), lambda s: (s, 0)),
            pl.BlockSpec((own_rows, tok_rows), lambda s: (0, s)),
            whole(own.shape),
            whole((own_rows, 1)),
        ],
        out_specs=(
            whole(own.shape),
            whole(own.shape),
            whole((own_rows, 1)),
            whole((own_rows, 1)),
        ),
        compiler_params=pltpu.CompilerParams(vmem_limit_bytes=48 * 2**20),
        cost_estimate=pl.CostEstimate(
            flops=4 * feats.shape[0] * own_rows * width_all,
            bytes_accessed=30 * 2**20,
            transcendentals=feats.shape[0] * own_rows,
        ),
    )(own, far, feats, change, mom_own, second_col)


def update_kernel(order, far_ref, lead_ref, mixed_ref, rate_ref, *refs):
    param_ref, mom_ref = refs[-2:][::order]
    full = lead_ref[...] + (0.5 * BETA_ONE) * far_ref[...].astype(jnp.float32)
    mom_ref[...] = full.astype(mom_ref.dtype)
    param_ref[...] = (mixed_ref[...].astype(jnp.float32) - rate_ref[...] * full).astype(
        param_ref.dtype
    )


def update(first, far, lead, mixed, rate, before, order, block=64):
    rows, width_all = far.shape
    skip = first // block

    def cut(width, skip=skip):
        return pl.BlockSpec((block, width), lambda i: (skip + i, 0))

    whole = jax.ShapeDtypeStruct(lead.shape, jnp.bfloat16)
    held = () if before is None else tuple(before)
    return pl.pallas_call(
        partial(update_kernel, order),
        grid=(rows // block,),
        out_shape=(whole, whole),
        in_specs=[cut(width_all, 0), cut(width_all), cut(width_all), cut(1)]
        + [pl.BlockSpec(memory_space=pl.ANY)] * len(held),
        out_specs=(cut(width_all), cut(width_all)),
        input_output_aliases={4 + k: k for k in range(len(held))},
        compiler_params=pltpu.CompilerParams(vmem_limit_bytes=32 * 2**20),
        cost_estimate=pl.CostEstimate(
            flops=6 * rows * width_all, bytes_accessed=12 * rows * width_all, transcendentals=0
        ),
    )(far, lead, mixed, rate, *held)


def turned(value, axis, by):
    size = lax.axis_size(axis)
    return lax.ppermute(value, axis, [(i, (i + by) % size) for i in range(size)])


def step_at(token_codes, params, moments, second, distance):
    order = -1 if distance == 1 else 1
    groups = lax.axis_size("fsdp")
    tok_rows = token_codes.shape[1]
    own_rows, width_all = params.shape[1:]
    weights, mom_own = params[0], moments[0]

    codes = [token_codes] + [turned(token_codes, "fsdp", k) for k in range(1, groups)]
    weights_far = turned(weights, "dp", distance)
    pieces = 5
    rows = own_rows // pieces
    mom_far = [
        turned(mom_own[k * rows : (k + 1) * rows], "dp", distance) for k in range(pieces)
    ]

    codes = jnp.concatenate([c[0] for c in codes])
    first_col = lax.axis_index("fsdp") * own_rows
    feats, change = make_features(codes, first_col, tok_rows, own_rows, width_all)
    mixed, lead, *columns = make_gradient(
        weights, weights_far, feats, change, mom_own, second[0][:, None], tok_rows, order
    )
    second_new, rate = columns[::order]
    outs = None
    for k in range(pieces):
        outs = update(k * rows, mom_far[k], lead, mixed, rate, outs, order)
    param_new, mom_new = outs[::order]
    return (param_new[None], mom_new[None], second_new[:, 0][None])


def local(step_index, token_codes, params, moments, second):
    levels = min(5, lax.axis_size("dp").bit_length() - 1)
    branches = [partial(step_at, distance=2**power) for power in range(levels)]
    return lax.switch(step_index[0] % levels, branches, token_codes, params, moments, second)


def solution(mesh):
    in_specs = (P(), P("dp", "fsdp"), P("dp", "fsdp", None), P("dp", "fsdp", None), P("dp", "fsdp"))
    out_specs = (P("dp", "fsdp", None), P("dp", "fsdp", None), P("dp", "fsdp"))
    return jax.shard_map(local, mesh=mesh, in_specs=in_specs, out_specs=out_specs, check_vma=False)
```

```python
from functools import partial
import math

import jax
import jax.numpy as jnp
from jax import lax
from jax.experimental import pallas as pl
from jax.experimental.pallas import tpu as pltpu
from jax.sharding import PartitionSpec as P

GELU_SCALE = math.sqrt(2.0 / math.pi)
GELU_CUBIC = 0.044715
BETA_ONE = 0.9
BETA_TWO = 0.999
LEARN_RATE = 0.001
EPSILON = 1e-08
LANES = 128
BAND = 16


def turn_pair(turns):
    quarter = (turns + 8192) >> 14
    rest = (turns - (quarter << 14)).astype(jnp.float32) * (2.0 * math.pi / 65536.0)
    square = rest * rest
    sine = rest + rest * square * (
        -1.6666654611e-1 + square * (8.3321608736e-3 + square * -1.9515295891e-4)
    )
    cosine = (
        1.0
        - 0.5 * square
        + square * square * (4.166664568298827e-2 + square * (-1.388731625493765e-3 + square * 2.443315711809948e-5))
    )
    odd = (quarter & 1) == 1
    cos_size = jnp.where(odd, sine, cosine)
    sin_size = jnp.where(odd, cosine, sine)
    cos_minus = ((quarter + 1) & 2) == 2
    sin_minus = (quarter & 2) == 2
    return (jnp.where(cos_minus, -cos_size, cos_size), jnp.where(sin_minus, -sin_size, sin_size))


def features_kernel(first_ref, codes_ref, feats_ref, change_ref, near_ref, far_ref, band_ref, block_ref):
    tokens, width_all = feats_ref.shape
    own_rows = change_ref.shape[0]
    root = math.sqrt(2.0)
    row = jnp.broadcast_to(codes_ref[...], (LANES, tokens))

    code = row.T
    step = (2 * code + 977) & 65535
    lane = lax.broadcasted_iota(jnp.int32, (tokens, LANES), 1)
    near_ref[0], near_ref[1] = turn_pair((step * lane) & 65535)
    far_cos, far_sin = turn_pair((code + step * (lane * LANES)) & 65535)
    far_ref[0], far_ref[1] = far_cos * root, far_sin * root

    def some_tokens(k, _):
        rows = pl.ds(k * 32, 32)
        near_cos, near_sin = near_ref[0, rows, :], near_ref[1, rows, :]
        far_cos, far_sin = far_ref[0, rows, :], far_ref[1, rows, :]
        for a in range(width_all // LANES):
            feats_ref[rows, a * LANES : (a + 1) * LANES] = (
                far_cos[:, a : a + 1] * near_cos - far_sin[:, a : a + 1] * near_sin
            ).astype(feats_ref.dtype)
        return 0

    lax.fori_loop(0, tokens // 32, some_tokens, 0)

    blocks = own_rows // BAND
    band = lax.broadcasted_iota(jnp.int32, (BAND, tokens), 0)
    block = lax.broadcasted_iota(jnp.int32, (blocks, tokens), 0)
    step = (2 * row + 977) & 65535
    near_cos, near_sin = turn_pair((step[:BAND] * band) & 65535)
    far_cos, far_sin = turn_pair((row[:blocks] + step[:blocks] * (first_ref[0] + block * BAND)) & 65535)
    for k, value in enumerate((near_cos, near_sin)):
        band_ref[k], band_ref[2 + k] = value, pltpu.roll(value, tokens - 1, 1)
    for k, value in enumerate((far_cos * root, far_sin * root)):
        block_ref[k], block_ref[2 + k] = value, pltpu.roll(value, tokens - 1, 1)

    def some_rows(a, _):
        one = pl.ds(a, 1)
        here, there = (
            (block_ref[k, one, :] * band_ref[k] - block_ref[k + 1, one, :] * band_ref[k + 1])
            .astype(feats_ref.dtype)
            .astype(jnp.float32)
            for k in (0, 2)
        )
        change_ref[pl.ds(pl.multiple_of(a * BAND, BAND), BAND), :] = here - there
        return 0

    lax.fori_loop(0, blocks, some_rows, 0, unroll=4)


def make_features(codes, first_col, tok_rows, own_rows, width_all):
    count = codes.shape[0]
    return pl.pallas_call(
        features_kernel,
        grid=(count,),
        out_shape=(
            jax.ShapeDtypeStruct((count * tok_rows, width_all), jnp.bfloat16),
            jax.ShapeDtypeStruct((own_rows, count * tok_rows), jnp.float32),
        ),
        in_specs=[
            pl.BlockSpec(memory_space=pltpu.SMEM),
            pl.BlockSpec((None, 1, tok_rows), lambda s: (s, 0, 0)),
        ],
        out_specs=(
            pl.BlockSpec((tok_rows, width_all), lambda s: (s, 0)),
            pl.BlockSpec((own_rows, tok_rows), lambda s: (0, s)),
        ),
        scratch_shapes=[
            pltpu.VMEM((2, tok_rows, LANES), jnp.float32),
            pltpu.VMEM((2, tok_rows, LANES), jnp.float32),
            pltpu.VMEM((4, BAND, tok_rows), jnp.float32),
            pltpu.VMEM((4, own_rows // BAND, tok_rows), jnp.float32),
        ],
        compiler_params=pltpu.CompilerParams(vmem_limit_bytes=32 * 2**20),
        cost_estimate=pl.CostEstimate(
            flops=12 * 10**9, bytes_accessed=8 * 2**20, transcendentals=0
        ),
    )(first_col.reshape(1), codes[:, None, :])


def gradient_kernel(order, own_ref, far_ref, feats_ref, change_ref, mom_ref, second_ref, mixed_ref, lead_ref, *refs):
    new_ref, rate_ref = refs[:2][::order]
    error_ref, column_ref = refs[2:]
    sequence = pl.program_id(0)
    own_rows, width_all = own_ref.shape
    tokens = feats_ref.shape[0]

    @pl.when(sequence == 0)
    def _():
        def mix(k, _):
            rows = pl.ds(pl.multiple_of(k * 16, 16), 16)
            mixed_ref[rows, :] = (
                0.5 * (own_ref[rows, :].astype(jnp.float32) + far_ref[rows, :].astype(jnp.float32))
            ).astype(mixed_ref.dtype)
            lead_ref[rows, :] = jnp.zeros((16, width_all), jnp.float32)
            return 0

        lax.fori_loop(0, own_rows // 16, mix, 0)

    half = own_rows // 2

    def forward(k, _):
        rows = pl.ds(pl.multiple_of(k * half, half), half)
        hidden = lax.dot_general(
            mixed_ref[rows, :], feats_ref[...], (((1,), (1,)), ((), ())), preferred_element_type=jnp.float32
        )
        squared = hidden * hidden
        tangent = jnp.tanh(GELU_SCALE * hidden * (1.0 + GELU_CUBIC * squared))
        value = 0.5 * hidden * (1.0 + tangent)
        slope = 0.5 * (1.0 + tangent) + 0.5 * hidden * (1.0 - tangent * tangent) * GELU_SCALE * (
            1.0 + 3.0 * GELU_CUBIC * squared
        )
        keep = lax.broadcasted_iota(jnp.int32, (half, tokens), 1) < tokens - 1
        error_ref[rows, :] = jnp.where(keep, (change_ref[rows, :] + value) * slope, 0.0).astype(
            error_ref.dtype
        )
        return 0

    lax.fori_loop(0, 2, forward, 0)

    def backward(k, _):
        cut = pl.ds(pl.multiple_of(k * 256, 256), 256)
        term = lax.dot_general(
            error_ref[...], feats_ref[:, cut], (((1,), (0,)), ((), ())), preferred_element_type=jnp.float32
        )
        term = term.astype(jnp.bfloat16).astype(jnp.float32)
        lead_ref[:, cut] = lead_ref[:, cut] + term
        return 0

    lax.fori_loop(0, width_all // 256, backward, 0)

    @pl.when(sequence == pl.num_programs(0) - 1)
    def _():
        def finish(k, _):
            rows = pl.ds(pl.multiple_of(k * 16, 16), 16)
            sums = jnp.zeros((16, LANES), jnp.float32)
            for low in range(0, width_all, LANES):
                grad = lead_ref[rows, low : low + LANES]
                sums += grad * grad
                lead_ref[rows, low : low + LANES] = (0.5 * BETA_ONE) * mom_ref[
                    rows, low : low + LANES
                ].astype(jnp.float32) + (1.0 - BETA_ONE) * grad
            column_ref[rows, :] = sums
            return 0

        lax.fori_loop(0, own_rows // 16, finish, 0)
        mean = jnp.sum(column_ref[...].T, axis=0, keepdims=True) / width_all
        second_new = BETA_TWO * second_ref[...] + (1.0 - BETA_TWO) * mean
        new_ref[...] = second_new
        rate = LEARN_RATE / (jnp.sqrt(second_new) + EPSILON)
        rate_ref[...] = jnp.broadcast_to(rate, (LANES, own_rows)).T[:, :1]


def make_gradient(own, far, feats, change, mom_own, second, tok_rows, order):
    own_rows, width_all = own.shape
    groups = feats.shape[0] // tok_rows

    shapes = (own.shape, own.shape) + ((1, own_rows), (own_rows, 1))[::order]
    types = (jnp.bfloat16, jnp.float32, jnp.float32, jnp.float32)

    def whole(shape):
        return pl.BlockSpec(shape, lambda s: (0, 0), pipeline_mode=pl.Buffered(1))

    return pl.pallas_call(
        partial(gradient_kernel, order),
        grid=(groups,),
        out_shape=tuple(jax.ShapeDtypeStruct(s, t) for s, t in zip(shapes, types)),
        in_specs=[
            whole(own.shape),
            whole(own.shape),
            pl.BlockSpec((tok_rows, width_all), lambda s: (s, 0)),
            pl.BlockSpec((own_rows, tok_rows), lambda s: (0, s)),
            whole(own.shape),
            whole((1, own_rows)),
        ],
        out_specs=tuple(whole(s) for s in shapes),
        scratch_shapes=[
            pltpu.VMEM((own_rows, tok_rows), jnp.bfloat16),
            pltpu.VMEM((own_rows, LANES), jnp.float32),
        ],
        compiler_params=pltpu.CompilerParams(vmem_limit_bytes=48 * 2**20),
        cost_estimate=pl.CostEstimate(
            flops=30 * 10**9,
            bytes_accessed=30 * 2**20,
            transcendentals=feats.shape[0] * own_rows,
        ),
    )(own, far, feats, change, mom_own, second)


def update_kernel(order, far_ref, lead_ref, mixed_ref, rate_ref, *refs):
    param_ref, mom_ref = refs[-2:][::order]

    def some_rows(k, _):
        rows = pl.ds(pl.multiple_of(k * 16, 16), 16)
        full = lead_ref[rows, :] + (0.5 * BETA_ONE) * far_ref[rows, :].astype(jnp.float32)
        mom_ref[rows, :] = full.astype(mom_ref.dtype)
        param_ref[rows, :] = (
            mixed_ref[rows, :].astype(jnp.float32) - rate_ref[rows, :] * full
        ).astype(param_ref.dtype)
        return 0

    lax.fori_loop(0, far_ref.shape[0] // 16, some_rows, 0)


def update(first, far, lead, mixed, rate, before, order):
    rows, width_all = far.shape
    block = max(b for b in range(16, 161, 16) if rows % b == 0 and first % b == 0)
    skip = first // block

    def cut(width, skip=skip):
        return pl.BlockSpec((block, width), lambda i: (skip + i, 0))

    whole = jax.ShapeDtypeStruct(lead.shape, jnp.bfloat16)
    held = () if before is None else tuple(before)
    return pl.pallas_call(
        partial(update_kernel, order),
        grid=(rows // block,),
        out_shape=(whole, whole),
        in_specs=[cut(width_all, 0), cut(width_all), cut(width_all), cut(1)]
        + [pl.BlockSpec(memory_space=pl.ANY)] * len(held),
        out_specs=(cut(width_all), cut(width_all)),
        input_output_aliases={4 + k: k for k in range(len(held))},
        compiler_params=pltpu.CompilerParams(vmem_limit_bytes=32 * 2**20),
        cost_estimate=pl.CostEstimate(
            flops=6 * rows * width_all, bytes_accessed=12 * rows * width_all, transcendentals=0
        ),
    )(far, lead, mixed, rate, *held)


def turned(value, axis, by):
    size = lax.axis_size(axis)
    return lax.ppermute(value, axis, [(i, (i + by) % size) for i in range(size)])


def long_way(distance, size):
    hops = []
    for hop in range(3):
        pairs = []
        for i in range(size):
            ring, place = i // (4 * distance), i // distance % 4
            began = (place + hop) % 4
            carry = 1 if hop == 1 and began == 3 else 0
            there = (ring + carry) * 4 * distance + (place - 1) % 4 * distance + i % distance
            pairs.append((i, there % size))
        hops.append(pairs)
    return hops


def step_at(token_codes, params, moments, second, distance):
    order = -1 if distance == 1 else 1
    groups = lax.axis_size("fsdp")
    tok_rows = token_codes.shape[1]
    own_rows, width_all = params.shape[1:]
    weights, mom_own = params[0], moments[0]

    weights_far = turned(weights, "dp", distance)
    if distance <= 2:
        codes = jnp.concatenate(
            [token_codes] + [turned(token_codes, "fsdp", k) for k in range(1, groups)]
        )
    else:
        codes = lax.all_to_all(
            jnp.broadcast_to(token_codes, (groups, tok_rows)), "fsdp", 0, 0, tiled=True
        )
    first_col = lax.axis_index("fsdp") * own_rows
    relay = distance in (4, 16)
    if relay:
        starts = (0, own_rows * 9 // 20, own_rows * 3 // 4, own_rows)
    else:
        starts = (0, own_rows * 4 // 5, own_rows)
    mom_far = []
    feats, change = make_features(codes, first_col, tok_rows, own_rows, width_all)
    if relay:
        first, second_hop, last = long_way(distance, lax.axis_size("dp"))
        relayed = lax.ppermute(mom_own[: starts[1]], "dp", first)
        relayed = lax.ppermute(relayed, "dp", second_hop)
        relayed, feats, change = lax.optimization_barrier((relayed, feats, change))
        mom_far.append(lax.ppermute(relayed, "dp", last))
    done = len(mom_far)
    for low, high in zip(starts[done:], starts[done + 1 :]):
        mom_far.append(turned(mom_own[low:high], "dp", distance))

    mixed, lead, *columns = make_gradient(
        weights, weights_far, feats, change, mom_own, second, tok_rows, order
    )
    second_new, rate = columns[::order]
    outs = None
    for low, far in zip(starts, mom_far):
        outs = update(low, far, lead, mixed, rate, outs, order)
    param_new, mom_new = outs[::order]
    return (param_new[None], mom_new[None], second_new)


def local(step_index, token_codes, params, moments, second):
    levels = min(5, lax.axis_size("dp").bit_length() - 1)
    branches = [partial(step_at, distance=2**power) for power in range(levels)]
    return lax.switch(step_index[0] % levels, branches, token_codes, params, moments, second)


def solution(mesh):
    in_specs = (P(), P("dp", "fsdp"), P("dp", "fsdp", None), P("dp", "fsdp", None), P("dp", "fsdp"))
    out_specs = (P("dp", "fsdp", None), P("dp", "fsdp", None), P("dp", "fsdp"))
    return jax.shard_map(local, mesh=mesh, in_specs=in_specs, out_specs=out_specs, check_vma=False)
```

```python
from functools import partial
import math

import jax
import jax.numpy as jnp
from jax import lax
from jax.experimental import pallas as pl
from jax.experimental.pallas import tpu as pltpu
from jax.sharding import PartitionSpec as P

GELU_SCALE = math.sqrt(2.0 / math.pi)
GELU_CUBIC = 0.044715
BETA_ONE = 0.9
BETA_TWO = 0.999
LEARN_RATE = 0.001
EPSILON = 1e-08
LANES = 128
BAND = 16
TURNS = 4
TOKS = 32
SPLIT = (0, 9, 19, 35, 40)


def turn_pair(turns):
    quarter = (turns + 8192) >> 14
    rest = (turns - (quarter << 14)).astype(jnp.float32) * (2.0 * math.pi / 65536.0)
    square = rest * rest
    sine = rest + rest * square * (
        -1.6666654611e-1 + square * (8.3321608736e-3 + square * -1.9515295891e-4)
    )
    cosine = (
        1.0
        - 0.5 * square
        + square * square * (4.166664568298827e-2 + square * (-1.388731625493765e-3 + square * 2.443315711809948e-5))
    )
    odd = (quarter & 1) == 1
    cos_size = jnp.where(odd, sine, cosine)
    sin_size = jnp.where(odd, cosine, sine)
    cos_minus = ((quarter + 1) & 2) == 2
    sin_minus = (quarter & 2) == 2
    return (jnp.where(cos_minus, -cos_size, cos_size), jnp.where(sin_minus, -sin_size, sin_size))


def features_kernel(first_ref, codes_ref, feats_ref, change_ref, code_ref, band_ref, block_ref):
    tokens, width_all = feats_ref.shape
    own_rows = change_ref.shape[0]
    root = math.sqrt(2.0)
    row = jnp.broadcast_to(codes_ref[...], (LANES, tokens))

    code_ref[...] = row.T
    half = LANES // 2
    lane = lax.broadcasted_iota(jnp.int32, (TOKS, LANES), 1)
    size = jnp.where(lane < half, root, 1.0)

    def some_tokens(k, _):
        rows = pl.ds(pl.multiple_of(k * TOKS, TOKS), TOKS)
        code = code_ref[rows, :]
        step = (2 * code + 977) & 65535
        near_cos, near_sin = turn_pair((step * lane) & 65535)
        far_turns = jnp.where(lane < half, code + step * (lane * (TURNS * LANES)), step * ((lane - half) * LANES))
        far_cos, far_sin = turn_pair(far_turns & 65535)
        far_cos, far_sin = far_cos * size, far_sin * size
        near = [(near_cos, near_sin)]
        for q in range(half + 1, half + TURNS):
            by_cos, by_sin = far_cos[:, q : q + 1], far_sin[:, q : q + 1]
            near.append((near_cos * by_cos - near_sin * by_sin, near_sin * by_cos + near_cos * by_sin))
        for p in range(width_all // (TURNS * LANES)):
            by_cos, by_sin = far_cos[:, p : p + 1], far_sin[:, p : p + 1]
            for q, (one_cos, one_sin) in enumerate(near):
                low = (p * TURNS + q) * LANES
                feats_ref[rows, low : low + LANES] = (by_cos * one_cos - by_sin * one_sin).astype(
                    feats_ref.dtype
                )
        return 0

    lax.fori_loop(0, tokens // TOKS, some_tokens, 0)

    blocks = own_rows // BAND
    band = lax.broadcasted_iota(jnp.int32, (BAND, tokens), 0)
    block = lax.broadcasted_iota(jnp.int32, (blocks, tokens), 0)
    step = (2 * row + 977) & 65535
    near_cos, near_sin = turn_pair((step[:BAND] * band) & 65535)
    far_cos, far_sin = turn_pair((row[:blocks] + step[:blocks] * (first_ref[0] + block * BAND)) & 65535)
    for k, value in enumerate((near_cos, near_sin)):
        band_ref[k], band_ref[2 + k] = value, pltpu.roll(value, tokens - 1, 1)
    for k, value in enumerate((far_cos * root, far_sin * root)):
        block_ref[k], block_ref[2 + k] = value, pltpu.roll(value, tokens - 1, 1)

    def some_rows(a, _):
        one = pl.ds(a, 1)
        here, there = (
            (block_ref[k, one, :] * band_ref[k] - block_ref[k + 1, one, :] * band_ref[k + 1])
            .astype(feats_ref.dtype)
            .astype(jnp.float32)
            for k in (0, 2)
        )
        change_ref[pl.ds(pl.multiple_of(a * BAND, BAND), BAND), :] = here - there
        return 0

    lax.fori_loop(0, blocks, some_rows, 0, unroll=4)


def make_features(codes, first_col, tok_rows, own_rows, width_all):
    count = codes.shape[0]
    return pl.pallas_call(
        features_kernel,
        grid=(count,),
        out_shape=(
            jax.ShapeDtypeStruct((count * tok_rows, width_all), jnp.bfloat16),
            jax.ShapeDtypeStruct((own_rows, count * tok_rows), jnp.float32),
        ),
        in_specs=[
            pl.BlockSpec(memory_space=pltpu.SMEM),
            pl.BlockSpec((None, 1, tok_rows), lambda s: (s, 0, 0)),
        ],
        out_specs=(
            pl.BlockSpec((tok_rows, width_all), lambda s: (s, 0)),
            pl.BlockSpec((own_rows, tok_rows), lambda s: (0, s)),
        ),
        scratch_shapes=[
            pltpu.VMEM((tok_rows, LANES), jnp.int32),
            pltpu.VMEM((4, BAND, tok_rows), jnp.float32),
            pltpu.VMEM((4, own_rows // BAND, tok_rows), jnp.float32),
        ],
        compiler_params=pltpu.CompilerParams(vmem_limit_bytes=12 * 2**20),
        cost_estimate=pl.CostEstimate(
            flops=9 * 10**9, bytes_accessed=8 * 2**20, transcendentals=0
        ),
    )(first_col.reshape(1), codes[:, None, :])


def gradient_kernel(order, tile, own_ref, far_ref, feats_ref, change_ref, mom_ref, second_ref, mixed_ref, lead_ref, *refs):
    new_ref, rate_ref = refs[:2][::order]
    hidden_ref, error_ref, column_ref = refs[2:]
    sequence = pl.program_id(0)
    own_rows, width_all = own_ref.shape
    tokens = feats_ref.shape[0]

    @pl.when(sequence == 0)
    def _():
        def mix(k, _):
            rows = pl.ds(pl.multiple_of(k * 16, 16), 16)
            mixed_ref[rows, :] = (
                0.5 * (own_ref[rows, :].astype(jnp.float32) + far_ref[rows, :].astype(jnp.float32))
            ).astype(mixed_ref.dtype)
            lead_ref[rows, :] = jnp.zeros((16, width_all), jnp.float32)
            return 0

        lax.fori_loop(0, own_rows // 16, mix, 0)

    hidden_ref[...] = lax.dot_general(
        mixed_ref[...], feats_ref[...], (((1,), (1,)), ((), ())), preferred_element_type=jnp.float32
    )
    keep = lax.broadcasted_iota(jnp.int32, (32, tokens), 1) < tokens - 1

    def forward(k, _):
        rows = pl.ds(pl.multiple_of(k * 32, 32), 32)
        hidden = hidden_ref[rows, :]
        squared = hidden * hidden
        tangent = jnp.tanh(GELU_SCALE * hidden * (1.0 + GELU_CUBIC * squared))
        value = 0.5 * hidden * (1.0 + tangent)
        slope = 0.5 * (1.0 + tangent) + 0.5 * hidden * (1.0 - tangent * tangent) * GELU_SCALE * (
            1.0 + 3.0 * GELU_CUBIC * squared
        )
        error_ref[rows, :] = jnp.where(keep, (change_ref[rows, :] + value) * slope, 0.0).astype(
            error_ref.dtype
        )
        return 0

    lax.fori_loop(0, own_rows // 32, forward, 0)

    def backward(k, _):
        cut = pl.ds(pl.multiple_of(k * tile, tile), tile)
        term = lax.dot_general(
            error_ref[...], feats_ref[:, cut], (((1,), (0,)), ((), ())), preferred_element_type=jnp.float32
        )
        term = term.astype(jnp.bfloat16).astype(jnp.float32)
        lead_ref[:, cut] = lead_ref[:, cut] + term
        return 0

    lax.fori_loop(0, width_all // tile, backward, 0)

    @pl.when(sequence == pl.num_programs(0) - 1)
    def _():
        def finish(k, _):
            rows = pl.ds(pl.multiple_of(k * 16, 16), 16)
            sums = jnp.zeros((16, LANES), jnp.float32)
            for low in range(0, width_all, LANES):
                grad = lead_ref[rows, low : low + LANES]
                sums += grad * grad
                lead_ref[rows, low : low + LANES] = (0.5 * BETA_ONE) * mom_ref[
                    rows, low : low + LANES
                ].astype(jnp.float32) + (1.0 - BETA_ONE) * grad
            column_ref[rows, :] = sums
            return 0

        lax.fori_loop(0, own_rows // 16, finish, 0)
        mean = jnp.sum(column_ref[...].T, axis=0, keepdims=True) / width_all
        second_new = BETA_TWO * second_ref[...] + (1.0 - BETA_TWO) * mean
        new_ref[...] = second_new
        rate = LEARN_RATE / (jnp.sqrt(second_new) + EPSILON)
        rate_ref[...] = jnp.broadcast_to(rate, (LANES, own_rows)).T[:, :1]


def make_gradient(own, far, feats, change, mom_own, second, tok_rows, order, tile):
    own_rows, width_all = own.shape
    groups = feats.shape[0] // tok_rows

    shapes = (own.shape, own.shape) + ((1, own_rows), (own_rows, 1))[::order]
    types = (jnp.bfloat16, jnp.float32, jnp.float32, jnp.float32)

    def whole(shape):
        return pl.BlockSpec(shape, lambda s: (0, 0), pipeline_mode=pl.Buffered(1))

    return pl.pallas_call(
        partial(gradient_kernel, order, tile),
        grid=(groups,),
        out_shape=tuple(jax.ShapeDtypeStruct(s, t) for s, t in zip(shapes, types)),
        in_specs=[
            whole(own.shape),
            whole(own.shape),
            pl.BlockSpec((tok_rows, width_all), lambda s: (s, 0)),
            pl.BlockSpec((own_rows, tok_rows), lambda s: (0, s)),
            whole(own.shape),
            whole((1, own_rows)),
        ],
        out_specs=tuple(whole(s) for s in shapes),
        scratch_shapes=[
            pltpu.VMEM((own_rows, tok_rows), jnp.float32),
            pltpu.VMEM((own_rows, tok_rows), jnp.bfloat16),
            pltpu.VMEM((own_rows, LANES), jnp.float32),
        ],
        compiler_params=pltpu.CompilerParams(vmem_limit_bytes=30 * 2**20),
        cost_estimate=pl.CostEstimate(
            flops=30 * 10**9,
            bytes_accessed=30 * 2**20,
            transcendentals=feats.shape[0] * own_rows,
        ),
    )(own, far, feats, change, mom_own, second)


def update_kernel(order, far_ref, lead_ref, mixed_ref, rate_ref, *refs):
    param_ref, mom_ref = refs[-2:][::order]

    def some_rows(k, _):
        rows = pl.ds(pl.multiple_of(k * 16, 16), 16)
        full = lead_ref[rows, :] + (0.5 * BETA_ONE) * far_ref[rows, :].astype(jnp.float32)
        mom_ref[rows, :] = full.astype(mom_ref.dtype)
        param_ref[rows, :] = (
            mixed_ref[rows, :].astype(jnp.float32) - rate_ref[rows, :] * full
        ).astype(param_ref.dtype)
        return 0

    lax.fori_loop(0, far_ref.shape[0] // 16, some_rows, 0)


def update(first, far, lead, mixed, rate, before, order):
    rows, width_all = far.shape
    block = max(b for b in range(16, 97, 16) if rows % b == 0)

    def piece(width):
        return pl.BlockSpec((pl.Element(block), pl.Element(width)), lambda i: ((first // 16 + i * (block // 16)) * 16, 0))

    whole = jax.ShapeDtypeStruct(lead.shape, jnp.bfloat16)
    held = () if before is None else tuple(before)
    return pl.pallas_call(
        partial(update_kernel, order),
        grid=(rows // block,),
        out_shape=(whole, whole),
        in_specs=[pl.BlockSpec((block, width_all), lambda i: (i, 0)), piece(width_all), piece(width_all), piece(1)]
        + [pl.BlockSpec(memory_space=pl.ANY)] * len(held),
        out_specs=(piece(width_all), piece(width_all)),
        input_output_aliases={4 + k: k for k in range(len(held))},
        compiler_params=pltpu.CompilerParams(vmem_limit_bytes=20 * 2**20),
        cost_estimate=pl.CostEstimate(
            flops=6 * rows * width_all, bytes_accessed=12 * rows * width_all, transcendentals=0
        ),
    )(far, lead, mixed, rate, *held)


def turned(value, axis, by):
    size = lax.axis_size(axis)
    return lax.ppermute(value, axis, [(i, (i + by) % size) for i in range(size)])


def after(value, *others):
    return lax.optimization_barrier((value, *others))[0]


def long_way(distance, size):
    hops = []
    for hop in range(3):
        pairs = []
        for i in range(size):
            ring, place = i // (4 * distance), i // distance % 4
            began = (place + hop) % 4
            carry = 1 if hop == 1 and began == 3 else 0
            there = (ring + carry) * 4 * distance + (place - 1) % 4 * distance + i % distance
            pairs.append((i, there % size))
        hops.append(pairs)
    return hops


def step_at(token_codes, params, moments, second, distance):
    order = -1 if distance == 1 else 1
    groups = lax.axis_size("fsdp")
    tok_rows = token_codes.shape[1]
    own_rows, width_all = params.shape[1:]
    weights, mom_own = params[0], moments[0]

    weights_far = turned(weights, "dp", distance)
    relay = distance in (4, 16)
    if relay:
        starts = tuple(own_rows * k // 40 for k in SPLIT)
    elif distance == 1:
        starts = tuple(own_rows * k // 10 for k in (0, 8, 10))
    else:
        starts = tuple(own_rows * k // 10 for k in (0, 9, 10))
    mom_own_parts = []
    for low, high in zip(starts, starts[1:]):
        whole = after(mom_own, mom_own_parts[-1]) if relay and len(mom_own_parts) >= 2 else mom_own
        mom_own_parts.append(whole[low:high])
    if distance <= 2:
        codes = jnp.concatenate(
            [token_codes] + [turned(token_codes, "fsdp", k) for k in range(1, groups)]
        )
    else:
        own_codes = after(token_codes, mom_own_parts[2]) if relay else token_codes
        codes = lax.all_to_all(
            jnp.broadcast_to(own_codes, (groups, tok_rows)), "fsdp", 0, 0, tiled=True
        )
    first_col = lax.axis_index("fsdp") * own_rows
    mom_far = []
    feats, change = make_features(codes, first_col, tok_rows, own_rows, width_all)
    if relay:
        first, second_hop, last = long_way(distance, lax.axis_size("dp"))
        one, two = (lax.ppermute(part, "dp", first) for part in mom_own_parts[:2])
        one_next = lax.ppermute(one, "dp", second_hop)
        two_next = lax.ppermute(after(two, one), "dp", second_hop)
        mom_far.append(lax.ppermute(one_next, "dp", last))
        mom_far.append(lax.ppermute(after(two_next, one_next, feats, change), "dp", last))
    for part in mom_own_parts[len(mom_far) :]:
        mom_far.append(turned(part, "dp", distance))

    mixed, lead, *columns = make_gradient(
        weights, weights_far, feats, change, mom_own, second, tok_rows, order, width_all // 2 if distance == 1 else 256
    )
    second_new, rate = columns[::order]
    outs = None
    pieces = list(zip(starts, mom_far))
    if relay:
        pieces[1], pieces[2] = pieces[2], pieces[1]
    for low, far in pieces:
        outs = update(low, far, lead, mixed, rate, outs, order)
    param_new, mom_new = outs[::order]
    return (param_new[None], mom_new[None], second_new)


def local(step_index, token_codes, params, moments, second):
    levels = min(5, lax.axis_size("dp").bit_length() - 1)
    branches = [partial(step_at, distance=2**power) for power in range(levels)]
    return lax.switch(step_index[0] % levels, branches, token_codes, params, moments, second)


def solution(mesh):
    in_specs = (P(), P("dp", "fsdp"), P("dp", "fsdp", None), P("dp", "fsdp", None), P("dp", "fsdp"))
    out_specs = (P("dp", "fsdp", None), P("dp", "fsdp", None), P("dp", "fsdp"))
    return jax.shard_map(local, mesh=mesh, in_specs=in_specs, out_specs=out_specs, check_vma=False)
```

```python
from functools import partial
import math

import jax
import jax.numpy as jnp
from jax import lax
from jax.experimental import pallas as pl
from jax.experimental.pallas import tpu as pltpu
from jax.sharding import PartitionSpec as P

GELU_SCALE = math.sqrt(2.0 / math.pi)
GELU_CUBIC = 0.044715
BETA_ONE = 0.9
BETA_TWO = 0.999
LEARN_RATE = 0.001
EPSILON = 1e-08
LANES = 128
BAND = 16
TURNS = 4
TOKS = 32
SPLIT = (0, 9, 19, 35, 40)


def turn_pair(turns):
    quarter = (turns + 8192) >> 14
    rest = (turns - (quarter << 14)).astype(jnp.float32) * (2.0 * math.pi / 65536.0)
    square = rest * rest
    sine = rest + rest * square * (
        -1.6666654611e-1 + square * (8.3321608736e-3 + square * -1.9515295891e-4)
    )
    cosine = (
        1.0
        - 0.5 * square
        + square * square * (4.166664568298827e-2 + square * (-1.388731625493765e-3 + square * 2.443315711809948e-5))
    )
    odd = (quarter & 1) == 1
    cos_size = jnp.where(odd, sine, cosine)
    sin_size = jnp.where(odd, cosine, sine)
    cos_minus = ((quarter + 1) & 2) == 2
    sin_minus = (quarter & 2) == 2
    return (jnp.where(cos_minus, -cos_size, cos_size), jnp.where(sin_minus, -sin_size, sin_size))


def features_kernel(first_ref, codes_ref, feats_ref, change_ref, code_ref, band_ref, block_ref):
    tokens, width_all = feats_ref.shape
    own_rows = change_ref.shape[0]
    root = math.sqrt(2.0)
    row = jnp.broadcast_to(codes_ref[...], (LANES, tokens))

    code_ref[...] = row.T
    half = LANES // 2
    lane = lax.broadcasted_iota(jnp.int32, (TOKS, LANES), 1)
    size = jnp.where(lane < half, root, 1.0)

    def some_tokens(k, _):
        rows = pl.ds(pl.multiple_of(k * TOKS, TOKS), TOKS)
        code = code_ref[rows, :]
        step = (2 * code + 977) & 65535
        near_cos, near_sin = turn_pair((step * lane) & 65535)
        far_turns = jnp.where(lane < half, code + step * (lane * (TURNS * LANES)), step * ((lane - half) * LANES))
        far_cos, far_sin = turn_pair(far_turns & 65535)
        far_cos, far_sin = far_cos * size, far_sin * size
        near = [(near_cos, near_sin)]
        for q in range(half + 1, half + TURNS):
            by_cos, by_sin = far_cos[:, q : q + 1], far_sin[:, q : q + 1]
            near.append((near_cos * by_cos - near_sin * by_sin, near_sin * by_cos + near_cos * by_sin))
        for p in range(width_all // (TURNS * LANES)):
            by_cos, by_sin = far_cos[:, p : p + 1], far_sin[:, p : p + 1]
            for q, (one_cos, one_sin) in enumerate(near):
                low = (p * TURNS + q) * LANES
                feats_ref[rows, low : low + LANES] = (by_cos * one_cos - by_sin * one_sin).astype(
                    feats_ref.dtype
                )
        return 0

    lax.fori_loop(0, tokens // TOKS, some_tokens, 0)

    blocks = own_rows // BAND
    band = lax.broadcasted_iota(jnp.int32, (BAND, tokens), 0)
    block = lax.broadcasted_iota(jnp.int32, (blocks, tokens), 0)
    step = (2 * row + 977) & 65535
    near_cos, near_sin = turn_pair((step[:BAND] * band) & 65535)
    far_cos, far_sin = turn_pair((row[:blocks] + step[:blocks] * (first_ref[0] + block * BAND)) & 65535)
    for k, value in enumerate((near_cos, near_sin)):
        band_ref[k], band_ref[2 + k] = value, pltpu.roll(value, tokens - 1, 1)
    for k, value in enumerate((far_cos * root, far_sin * root)):
        block_ref[k], block_ref[2 + k] = value, pltpu.roll(value, tokens - 1, 1)

    def some_rows(a, _):
        one = pl.ds(a, 1)
        here, there = (
            (block_ref[k, one, :] * band_ref[k] - block_ref[k + 1, one, :] * band_ref[k + 1])
            .astype(feats_ref.dtype)
            .astype(jnp.float32)
            for k in (0, 2)
        )
        change_ref[pl.ds(pl.multiple_of(a * BAND, BAND), BAND), :] = here - there
        return 0

    lax.fori_loop(0, blocks, some_rows, 0, unroll=4)


def make_features(codes, first_col, tok_rows, own_rows, width_all):
    count = codes.shape[0]
    return pl.pallas_call(
        features_kernel,
        grid=(count,),
        out_shape=(
            jax.ShapeDtypeStruct((count * tok_rows, width_all), jnp.bfloat16),
            jax.ShapeDtypeStruct((own_rows, count * tok_rows), jnp.float32),
        ),
        in_specs=[
            pl.BlockSpec(memory_space=pltpu.SMEM),
            pl.BlockSpec((None, 1, tok_rows), lambda s: (s, 0, 0)),
        ],
        out_specs=(
            pl.BlockSpec((tok_rows, width_all), lambda s: (s, 0)),
            pl.BlockSpec((own_rows, tok_rows), lambda s: (0, s)),
        ),
        scratch_shapes=[
            pltpu.VMEM((tok_rows, LANES), jnp.int32),
            pltpu.VMEM((4, BAND, tok_rows), jnp.float32),
            pltpu.VMEM((4, own_rows // BAND, tok_rows), jnp.float32),
        ],
        compiler_params=pltpu.CompilerParams(vmem_limit_bytes=12 * 2**20),
        cost_estimate=pl.CostEstimate(
            flops=9 * 10**9, bytes_accessed=8 * 2**20, transcendentals=0
        ),
    )(first_col.reshape(1), codes[:, None, :])


def gradient_kernel(order, tile, own_ref, far_ref, feats_ref, change_ref, mom_ref, second_ref, mixed_ref, lead_ref, *refs):
    new_ref, rate_ref = refs[:2][::order]
    hidden_ref, error_ref, column_ref = refs[2:]
    sequence = pl.program_id(0)
    own_rows, width_all = own_ref.shape
    tokens = feats_ref.shape[0]

    @pl.when(sequence == 0)
    def _():
        def mix(k, _):
            rows = pl.ds(pl.multiple_of(k * 16, 16), 16)
            mixed_ref[rows, :] = (
                0.5 * (own_ref[rows, :].astype(jnp.float32) + far_ref[rows, :].astype(jnp.float32))
            ).astype(mixed_ref.dtype)
            lead_ref[rows, :] = jnp.zeros((16, width_all), jnp.float32)
            return 0

        lax.fori_loop(0, own_rows // 16, mix, 0)

    hidden_ref[...] = lax.dot_general(
        mixed_ref[...], feats_ref[...], (((1,), (1,)), ((), ())), preferred_element_type=jnp.float32
    )
    keep = lax.broadcasted_iota(jnp.int32, (32, tokens), 1) < tokens - 1

    def forward(k, _):
        rows = pl.ds(pl.multiple_of(k * 32, 32), 32)
        hidden = hidden_ref[rows, :]
        squared = hidden * hidden
        tangent = jnp.tanh(GELU_SCALE * hidden * (1.0 + GELU_CUBIC * squared))
        value = 0.5 * hidden * (1.0 + tangent)
        slope = 0.5 * (1.0 + tangent) + 0.5 * hidden * (1.0 - tangent * tangent) * GELU_SCALE * (
            1.0 + 3.0 * GELU_CUBIC * squared
        )
        error_ref[rows, :] = jnp.where(keep, (change_ref[rows, :] + value) * slope, 0.0).astype(
            error_ref.dtype
        )
        return 0

    lax.fori_loop(0, own_rows // 32, forward, 0)

    def backward(k, _):
        cut = pl.ds(pl.multiple_of(k * tile, tile), tile)
        term = lax.dot_general(
            error_ref[...], feats_ref[:, cut], (((1,), (0,)), ((), ())), preferred_element_type=jnp.float32
        )
        term = term.astype(jnp.bfloat16).astype(jnp.float32)
        lead_ref[:, cut] = lead_ref[:, cut] + term
        return 0

    lax.fori_loop(0, width_all // tile, backward, 0)

    @pl.when(sequence == pl.num_programs(0) - 1)
    def _():
        def finish(k, _):
            rows = pl.ds(pl.multiple_of(k * 16, 16), 16)
            sums = jnp.zeros((16, LANES), jnp.float32)
            for low in range(0, width_all, LANES):
                grad = lead_ref[rows, low : low + LANES]
                sums += grad * grad
                lead_ref[rows, low : low + LANES] = (0.5 * BETA_ONE) * mom_ref[
                    rows, low : low + LANES
                ].astype(jnp.float32) + (1.0 - BETA_ONE) * grad
            column_ref[rows, :] = sums
            return 0

        lax.fori_loop(0, own_rows // 16, finish, 0)
        mean = jnp.sum(column_ref[...].T, axis=0, keepdims=True) / width_all
        second_new = BETA_TWO * second_ref[...] + (1.0 - BETA_TWO) * mean
        new_ref[...] = second_new
        rate = LEARN_RATE / (jnp.sqrt(second_new) + EPSILON)
        rate_ref[...] = jnp.broadcast_to(rate, (LANES, own_rows)).T[:, :1]


def make_gradient(own, far, feats, change, mom_own, second, tok_rows, order, tile):
    own_rows, width_all = own.shape
    groups = feats.shape[0] // tok_rows

    shapes = (own.shape, own.shape) + ((1, own_rows), (own_rows, 1))[::order]
    types = (jnp.bfloat16, jnp.float32, jnp.float32, jnp.float32)

    def whole(shape):
        return pl.BlockSpec(shape, lambda s: (0, 0), pipeline_mode=pl.Buffered(1))

    return pl.pallas_call(
        partial(gradient_kernel, order, tile),
        grid=(groups,),
        out_shape=tuple(jax.ShapeDtypeStruct(s, t) for s, t in zip(shapes, types)),
        in_specs=[
            whole(own.shape),
            whole(own.shape),
            pl.BlockSpec((tok_rows, width_all), lambda s: (s, 0)),
            pl.BlockSpec((own_rows, tok_rows), lambda s: (0, s)),
            whole(own.shape),
            whole((1, own_rows)),
        ],
        out_specs=tuple(whole(s) for s in shapes),
        scratch_shapes=[
            pltpu.VMEM((own_rows, tok_rows), jnp.float32),
            pltpu.VMEM((own_rows, tok_rows), jnp.bfloat16),
            pltpu.VMEM((own_rows, LANES), jnp.float32),
        ],
        compiler_params=pltpu.CompilerParams(vmem_limit_bytes=30 * 2**20),
        cost_estimate=pl.CostEstimate(
            flops=30 * 10**9,
            bytes_accessed=30 * 2**20,
            transcendentals=feats.shape[0] * own_rows,
        ),
    )(own, far, feats, change, mom_own, second)


def update_kernel(order, far_ref, lead_ref, mixed_ref, rate_ref, *refs):
    param_ref, mom_ref = refs[-2:][::order]

    def some_rows(k, _):
        rows = pl.ds(pl.multiple_of(k * 16, 16), 16)
        full = lead_ref[rows, :] + (0.5 * BETA_ONE) * far_ref[rows, :].astype(jnp.float32)
        mom_ref[rows, :] = full.astype(mom_ref.dtype)
        param_ref[rows, :] = (
            mixed_ref[rows, :].astype(jnp.float32) - rate_ref[rows, :] * full
        ).astype(param_ref.dtype)
        return 0

    lax.fori_loop(0, far_ref.shape[0] // 16, some_rows, 0)


def update(first, far, lead, mixed, rate, before, order):
    rows, width_all = far.shape
    block = max(b for b in range(16, 97, 16) if rows % b == 0)

    def piece(width):
        return pl.BlockSpec((pl.Element(block), pl.Element(width)), lambda i: ((first // 16 + i * (block // 16)) * 16, 0))

    whole = jax.ShapeDtypeStruct(lead.shape, jnp.bfloat16)
    held = () if before is None else tuple(before)
    return pl.pallas_call(
        partial(update_kernel, order),
        grid=(rows // block,),
        out_shape=(whole, whole),
        in_specs=[pl.BlockSpec((block, width_all), lambda i: (i, 0)), piece(width_all), piece(width_all), piece(1)]
        + [pl.BlockSpec(memory_space=pl.ANY)] * len(held),
        out_specs=(piece(width_all), piece(width_all)),
        input_output_aliases={4 + k: k for k in range(len(held))},
        compiler_params=pltpu.CompilerParams(vmem_limit_bytes=20 * 2**20),
        cost_estimate=pl.CostEstimate(
            flops=6 * rows * width_all, bytes_accessed=12 * rows * width_all, transcendentals=0
        ),
    )(far, lead, mixed, rate, *held)


def turned(value, axis, by):
    size = lax.axis_size(axis)
    return lax.ppermute(value, axis, [(i, (i + by) % size) for i in range(size)])


def after(value, *others):
    return lax.optimization_barrier((value, *others))[0]


def long_way(distance, size):
    hops = []
    for hop in range(3):
        pairs = []
        for i in range(size):
            ring, place = i // (4 * distance), i // distance % 4
            began = (place + hop) % 4
            carry = 1 if hop == 1 and began == 3 else 0
            there = (ring + carry) * 4 * distance + (place - 1) % 4 * distance + i % distance
            pairs.append((i, there % size))
        hops.append(pairs)
    return hops


def step_at(token_codes, params, moments, second, distance):
    order = -1 if distance == 1 else 1
    groups = lax.axis_size("fsdp")
    tok_rows = token_codes.shape[1]
    own_rows, width_all = params.shape[1:]
    weights, mom_own = params[0], moments[0]

    weights_far = turned(weights, "dp", distance)
    relay = distance in (4, 16)
    if relay:
        starts = tuple(own_rows * k // 40 for k in SPLIT)
    elif distance == 1:
        starts = tuple(own_rows * k // 10 for k in (0, 8, 10))
    else:
        starts = tuple(own_rows * k // 10 for k in (0, 9, 10))
    mom_own_parts = []
    for low, high in zip(starts, starts[1:]):
        whole = after(mom_own, mom_own_parts[-1]) if len(mom_own_parts) > relay else mom_own
        mom_own_parts.append(whole[low:high])
    if distance <= 2:
        codes = jnp.concatenate(
            [token_codes] + [turned(token_codes, "fsdp", k) for k in range(1, groups)]
        )
    else:
        own_codes = after(token_codes, mom_own_parts[2]) if relay else token_codes
        codes = lax.all_to_all(
            jnp.broadcast_to(own_codes, (groups, tok_rows)), "fsdp", 0, 0, tiled=True
        )
    first_col = lax.axis_index("fsdp") * own_rows
    mom_far = []
    feats, change = make_features(codes, first_col, tok_rows, own_rows, width_all)
    if relay:
        first, second_hop, last = long_way(distance, lax.axis_size("dp"))
        one, two = (lax.ppermute(part, "dp", first) for part in mom_own_parts[:2])
        one_next = lax.ppermute(one, "dp", second_hop)
        two_next = lax.ppermute(after(two, one), "dp", second_hop)
        mom_far.append(lax.ppermute(one_next, "dp", last))
        mom_far.append(lax.ppermute(after(two_next, one_next, feats, change), "dp", last))
    for part in mom_own_parts[len(mom_far) :]:
        mom_far.append(turned(part, "dp", distance))

    mixed, lead, *columns = make_gradient(
        weights, weights_far, feats, change, mom_own, second, tok_rows, order, width_all // 2 if distance == 1 else 256
    )
    second_new, rate = columns[::order]
    outs = None
    pieces = list(zip(starts, mom_far))
    if relay:
        pieces[1], pieces[2] = pieces[2], pieces[1]
    for low, far in pieces:
        outs = update(low, far, lead, mixed, rate, outs, order)
    param_new, mom_new = outs[::order]
    return (param_new[None], mom_new[None], second_new)


def local(step_index, token_codes, params, moments, second):
    levels = min(5, lax.axis_size("dp").bit_length() - 1)
    branches = [partial(step_at, distance=2**power) for power in range(levels)]
    return lax.switch(step_index[0] % levels, branches, token_codes, params, moments, second)


def solution(mesh):
    in_specs = (P(), P("dp", "fsdp"), P("dp", "fsdp", None), P("dp", "fsdp", None), P("dp", "fsdp"))
    out_specs = (P("dp", "fsdp", None), P("dp", "fsdp", None), P("dp", "fsdp"))
    return jax.shard_map(local, mesh=mesh, in_specs=in_specs, out_specs=out_specs, check_vma=False)
```

```python
from functools import partial
import math

import jax
import jax.numpy as jnp
from jax import lax
from jax.experimental import pallas as pl
from jax.experimental.pallas import tpu as pltpu
from jax.sharding import PartitionSpec as P

GELU_SCALE = math.sqrt(2.0 / math.pi)
GELU_CUBIC = 0.044715
BETA_ONE = 0.9
BETA_TWO = 0.999
LEARN_RATE = 0.001
EPSILON = 1e-08
LANES = 128
BAND = 16
TURNS = 4
TOKS = 32
SPLIT = (0, 9, 19, 37, 40)


def turn_pair(turns):
    quarter = (turns + 8192) >> 14
    rest = (turns - (quarter << 14)).astype(jnp.float32) * (2.0 * math.pi / 65536.0)
    square = rest * rest
    sine = rest + rest * square * (
        -1.6666654611e-1 + square * (8.3321608736e-3 + square * -1.9515295891e-4)
    )
    cosine = (
        1.0
        - 0.5 * square
        + square * square * (4.166664568298827e-2 + square * (-1.388731625493765e-3 + square * 2.443315711809948e-5))
    )
    odd = (quarter & 1) == 1
    cos_size = jnp.where(odd, sine, cosine)
    sin_size = jnp.where(odd, cosine, sine)
    cos_minus = ((quarter + 1) & 2) == 2
    sin_minus = (quarter & 2) == 2
    return (jnp.where(cos_minus, -cos_size, cos_size), jnp.where(sin_minus, -sin_size, sin_size))


def features_kernel(codes_ref, feats_ref, code_ref):
    tokens, width_all = feats_ref.shape
    root = math.sqrt(2.0)
    row = jnp.broadcast_to(codes_ref[...], (LANES, tokens))

    code_ref[...] = row.T
    half = LANES // 2
    lane = lax.broadcasted_iota(jnp.int32, (TOKS, LANES), 1)
    size = jnp.where(lane < half, root, 1.0)

    def some_tokens(k, _):
        rows = pl.ds(pl.multiple_of(k * TOKS, TOKS), TOKS)
        code = code_ref[rows, :]
        step = (2 * code + 977) & 65535
        near_cos, near_sin = turn_pair((step * lane) & 65535)
        far_turns = jnp.where(lane < half, code + step * (lane * (TURNS * LANES)), step * ((lane - half) * LANES))
        far_cos, far_sin = turn_pair(far_turns & 65535)
        far_cos, far_sin = far_cos * size, far_sin * size
        near = [(near_cos, near_sin)]
        for q in range(half + 1, half + TURNS):
            by_cos, by_sin = far_cos[:, q : q + 1], far_sin[:, q : q + 1]
            near.append((near_cos * by_cos - near_sin * by_sin, near_sin * by_cos + near_cos * by_sin))
        for p in range(width_all // (TURNS * LANES)):
            by_cos, by_sin = far_cos[:, p : p + 1], far_sin[:, p : p + 1]
            for q, (one_cos, one_sin) in enumerate(near):
                low = (p * TURNS + q) * LANES
                feats_ref[rows, low : low + LANES] = (by_cos * one_cos - by_sin * one_sin).astype(
                    feats_ref.dtype
                )
        return 0

    lax.fori_loop(0, tokens // TOKS, some_tokens, 0)


def change_kernel(first_ref, codes_ref, change_ref, band_ref, block_ref):
    own_rows, tokens = change_ref.shape
    root = math.sqrt(2.0)
    row = jnp.broadcast_to(codes_ref[...], (LANES, tokens))

    blocks = own_rows // BAND
    band = lax.broadcasted_iota(jnp.int32, (BAND, tokens), 0)
    block = lax.broadcasted_iota(jnp.int32, (blocks, tokens), 0)
    step = (2 * row + 977) & 65535
    near_cos, near_sin = turn_pair((step[:BAND] * band) & 65535)
    far_cos, far_sin = turn_pair((row[:blocks] + step[:blocks] * (first_ref[0] + block * BAND)) & 65535)
    for k, value in enumerate((near_cos, near_sin)):
        band_ref[k], band_ref[2 + k] = value, pltpu.roll(value, tokens - 1, 1)
    for k, value in enumerate((far_cos * root, far_sin * root)):
        block_ref[k], block_ref[2 + k] = value, pltpu.roll(value, tokens - 1, 1)

    def some_rows(a, _):
        one = pl.ds(a, 1)
        here, there = (
            (block_ref[k, one, :] * band_ref[k] - block_ref[k + 1, one, :] * band_ref[k + 1])
            .astype(jnp.bfloat16)
            .astype(jnp.float32)
            for k in (0, 2)
        )
        change_ref[pl.ds(pl.multiple_of(a * BAND, BAND), BAND), :] = here - there
        return 0

    lax.fori_loop(0, blocks, some_rows, 0, unroll=4)


def make_features(codes, width_all):
    count, tok_rows = codes.shape
    return pl.pallas_call(
        features_kernel,
        grid=(count,),
        out_shape=jax.ShapeDtypeStruct((count * tok_rows, width_all), jnp.bfloat16),
        in_specs=[pl.BlockSpec((None, 1, tok_rows), lambda s: (s, 0, 0))],
        out_specs=pl.BlockSpec((tok_rows, width_all), lambda s: (s, 0)),
        scratch_shapes=[pltpu.VMEM((tok_rows, LANES), jnp.int32)],
        compiler_params=pltpu.CompilerParams(vmem_limit_bytes=12 * 2**20),
        cost_estimate=pl.CostEstimate(
            flops=4 * 10**9, bytes_accessed=5 * 2**20, transcendentals=0
        ),
    )(codes[:, None, :])


def make_change(codes, first_col, own_rows):
    count, tok_rows = codes.shape
    return pl.pallas_call(
        change_kernel,
        grid=(count,),
        out_shape=jax.ShapeDtypeStruct((own_rows, count * tok_rows), jnp.float32),
        in_specs=[
            pl.BlockSpec(memory_space=pltpu.SMEM),
            pl.BlockSpec((None, 1, tok_rows), lambda s: (s, 0, 0)),
        ],
        out_specs=pl.BlockSpec((own_rows, tok_rows), lambda s: (0, s)),
        scratch_shapes=[
            pltpu.VMEM((4, BAND, tok_rows), jnp.float32),
            pltpu.VMEM((4, own_rows // BAND, tok_rows), jnp.float32),
        ],
        compiler_params=pltpu.CompilerParams(vmem_limit_bytes=12 * 2**20),
        cost_estimate=pl.CostEstimate(
            flops=4 * 10**9, bytes_accessed=3 * 2**20, transcendentals=0
        ),
    )(first_col.reshape(1), codes[:, None, :])


def gradient_kernel(order, tile, own_ref, far_ref, feats_ref, change_ref, mom_ref, second_ref, mixed_ref, lead_ref, *refs):
    new_ref, rate_ref = refs[:2][::order]
    hidden_ref, error_ref, column_ref = refs[2:]
    sequence = pl.program_id(0)
    own_rows, width_all = own_ref.shape
    tokens = feats_ref.shape[0]

    @pl.when(sequence == 0)
    def _():
        def mix(k, _):
            rows = pl.ds(pl.multiple_of(k * 16, 16), 16)
            mixed_ref[rows, :] = (
                0.5 * (own_ref[rows, :].astype(jnp.float32) + far_ref[rows, :].astype(jnp.float32))
            ).astype(mixed_ref.dtype)
            lead_ref[rows, :] = jnp.zeros((16, width_all), jnp.float32)
            return 0

        lax.fori_loop(0, own_rows // 16, mix, 0)

    hidden_ref[...] = lax.dot_general(
        mixed_ref[...], feats_ref[...], (((1,), (1,)), ((), ())), preferred_element_type=jnp.float32
    )
    keep = lax.broadcasted_iota(jnp.int32, (32, tokens), 1) < tokens - 1

    def forward(k, _):
        rows = pl.ds(pl.multiple_of(k * 32, 32), 32)
        hidden = hidden_ref[rows, :]
        squared = hidden * hidden
        tangent = jnp.tanh(GELU_SCALE * hidden * (1.0 + GELU_CUBIC * squared))
        value = 0.5 * hidden * (1.0 + tangent)
        slope = 0.5 * (1.0 + tangent) + 0.5 * hidden * (1.0 - tangent * tangent) * GELU_SCALE * (
            1.0 + 3.0 * GELU_CUBIC * squared
        )
        error_ref[rows, :] = jnp.where(keep, (change_ref[rows, :] + value) * slope, 0.0).astype(
            error_ref.dtype
        )
        return 0

    lax.fori_loop(0, own_rows // 32, forward, 0)

    def backward(k, _):
        cut = pl.ds(pl.multiple_of(k * tile, tile), tile)
        term = lax.dot_general(
            error_ref[...], feats_ref[:, cut], (((1,), (0,)), ((), ())), preferred_element_type=jnp.float32
        )
        term = term.astype(jnp.bfloat16).astype(jnp.float32)
        lead_ref[:, cut] = lead_ref[:, cut] + term
        return 0

    lax.fori_loop(0, width_all // tile, backward, 0)

    @pl.when(sequence == pl.num_programs(0) - 1)
    def _():
        def finish(k, _):
            rows = pl.ds(pl.multiple_of(k * 16, 16), 16)
            sums = jnp.zeros((16, LANES), jnp.float32)
            for low in range(0, width_all, LANES):
                grad = lead_ref[rows, low : low + LANES]
                sums += grad * grad
                lead_ref[rows, low : low + LANES] = (0.5 * BETA_ONE) * mom_ref[
                    rows, low : low + LANES
                ].astype(jnp.float32) + (1.0 - BETA_ONE) * grad
            column_ref[rows, :] = sums
            return 0

        lax.fori_loop(0, own_rows // 16, finish, 0)
        mean = jnp.sum(column_ref[...].T, axis=0, keepdims=True) / width_all
        second_new = BETA_TWO * second_ref[...] + (1.0 - BETA_TWO) * mean
        new_ref[...] = second_new
        rate = LEARN_RATE / (jnp.sqrt(second_new) + EPSILON)
        rate_ref[...] = jnp.broadcast_to(rate, (LANES, own_rows)).T[:, :1]


def make_gradient(own, far, feats, change, mom_own, second, tok_rows, order, tile):
    own_rows, width_all = own.shape
    groups = feats.shape[0] // tok_rows

    shapes = (own.shape, own.shape) + ((1, own_rows), (own_rows, 1))[::order]
    types = (jnp.bfloat16, jnp.float32, jnp.float32, jnp.float32)

    def whole(shape):
        return pl.BlockSpec(shape, lambda s: (0, 0), pipeline_mode=pl.Buffered(1))

    return pl.pallas_call(
        partial(gradient_kernel, order, tile),
        grid=(groups,),
        out_shape=tuple(jax.ShapeDtypeStruct(s, t) for s, t in zip(shapes, types)),
        in_specs=[
            whole(own.shape),
            whole(own.shape),
            pl.BlockSpec((tok_rows, width_all), lambda s: (s, 0)),
            pl.BlockSpec((own_rows, tok_rows), lambda s: (0, s)),
            whole(own.shape),
            whole((1, own_rows)),
        ],
        out_specs=tuple(whole(s) for s in shapes),
        scratch_shapes=[
            pltpu.VMEM((own_rows, tok_rows), jnp.float32),
            pltpu.VMEM((own_rows, tok_rows), jnp.bfloat16),
            pltpu.VMEM((own_rows, LANES), jnp.float32),
        ],
        compiler_params=pltpu.CompilerParams(vmem_limit_bytes=30 * 2**20),
        cost_estimate=pl.CostEstimate(
            flops=30 * 10**9,
            bytes_accessed=30 * 2**20,
            transcendentals=feats.shape[0] * own_rows,
        ),
    )(own, far, feats, change, mom_own, second)


def update_kernel(order, far_ref, lead_ref, mixed_ref, rate_ref, *refs):
    param_ref, mom_ref = refs[-2:][::order]

    def some_rows(k, _):
        rows = pl.ds(pl.multiple_of(k * 16, 16), 16)
        full = lead_ref[rows, :] + (0.5 * BETA_ONE) * far_ref[rows, :].astype(jnp.float32)
        mom_ref[rows, :] = full.astype(mom_ref.dtype)
        param_ref[rows, :] = (
            mixed_ref[rows, :].astype(jnp.float32) - rate_ref[rows, :] * full
        ).astype(param_ref.dtype)
        return 0

    lax.fori_loop(0, far_ref.shape[0] // 16, some_rows, 0)


def update(first, far, lead, mixed, rate, before, order):
    rows, width_all = far.shape
    block = max(b for b in range(16, 97, 16) if rows % b == 0)

    def piece(width):
        return pl.BlockSpec((pl.Element(block), pl.Element(width)), lambda i: ((first // 16 + i * (block // 16)) * 16, 0))

    whole = jax.ShapeDtypeStruct(lead.shape, jnp.bfloat16)
    held = () if before is None else tuple(before)
    return pl.pallas_call(
        partial(update_kernel, order),
        grid=(rows // block,),
        out_shape=(whole, whole),
        in_specs=[pl.BlockSpec((block, width_all), lambda i: (i, 0)), piece(width_all), piece(width_all), piece(1)]
        + [pl.BlockSpec(memory_space=pl.ANY)] * len(held),
        out_specs=(piece(width_all), piece(width_all)),
        input_output_aliases={4 + k: k for k in range(len(held))},
        compiler_params=pltpu.CompilerParams(vmem_limit_bytes=20 * 2**20),
        cost_estimate=pl.CostEstimate(
            flops=6 * rows * width_all, bytes_accessed=12 * rows * width_all, transcendentals=0
        ),
    )(far, lead, mixed, rate, *held)


def turned(value, axis, by):
    size = lax.axis_size(axis)
    return lax.ppermute(value, axis, [(i, (i + by) % size) for i in range(size)])


def after(value, *others):
    return lax.optimization_barrier((value, *others))[0]


def long_way(distance, size):
    hops = []
    for hop in range(3):
        pairs = []
        for i in range(size):
            ring, place = i // (4 * distance), i // distance % 4
            began = (place + hop) % 4
            carry = 1 if hop == 1 and began == 3 else 0
            there = (ring + carry) * 4 * distance + (place - 1) % 4 * distance + i % distance
            pairs.append((i, there % size))
        hops.append(pairs)
    return hops


def step_at(token_codes, params, moments, second, distance):
    order = -1 if distance == 1 else 1
    groups = lax.axis_size("fsdp")
    tok_rows = token_codes.shape[1]
    own_rows, width_all = params.shape[1:]
    weights, mom_own = params[0], moments[0]

    weights_far = turned(weights, "dp", distance)
    relay = distance in (4, 16)
    if relay:
        starts = tuple(own_rows * k // 40 for k in SPLIT)
    elif distance == 1:
        starts = tuple(own_rows * k // 10 for k in (0, 8, 10))
    else:
        starts = tuple(own_rows * k // 10 for k in (0, 9, 10))
    mom_own_parts = []
    for low, high in zip(starts, starts[1:]):
        whole = after(mom_own, mom_own_parts[-1]) if len(mom_own_parts) > relay else mom_own
        mom_own_parts.append(whole[low:high])
    if distance <= 2:
        codes = jnp.concatenate(
            [token_codes] + [turned(token_codes, "fsdp", k) for k in range(1, groups)]
        )
    else:
        own_codes = after(token_codes, mom_own_parts[2]) if relay else token_codes
        codes = lax.all_to_all(
            jnp.broadcast_to(own_codes, (groups, tok_rows)), "fsdp", 0, 0, tiled=True
        )
    first_col = lax.axis_index("fsdp") * own_rows
    mom_far = []
    if relay:
        first, second_hop, last = long_way(distance, lax.axis_size("dp"))
        one, two = (lax.ppermute(part, "dp", first) for part in mom_own_parts[:2])
        feats = make_features(after(codes, one), width_all)
        one = lax.ppermute(one, "dp", second_hop)
        two = lax.ppermute(after(two, feats), "dp", second_hop)
        change = make_change(after(codes, one), first_col, own_rows)
        mom_far.append(lax.ppermute(one, "dp", last))
        mom_far.append(lax.ppermute(after(two, change), "dp", last))
    else:
        feats = make_features(codes, width_all)
        change = make_change(codes, first_col, own_rows)
    for part in mom_own_parts[len(mom_far) :]:
        mom_far.append(turned(part, "dp", distance))

    mixed, lead, *columns = make_gradient(
        weights, weights_far, feats, change, mom_own, second, tok_rows, order, width_all // 2 if distance == 1 else 256
    )
    second_new, rate = columns[::order]
    outs = None
    for low, far in zip(starts, mom_far):
        outs = update(low, far, lead, mixed, rate, outs, order)
    param_new, mom_new = outs[::order]
    return (param_new[None], mom_new[None], second_new)


def local(step_index, token_codes, params, moments, second):
    levels = min(5, lax.axis_size("dp").bit_length() - 1)
    branches = [partial(step_at, distance=2**power) for power in range(levels)]
    return lax.switch(step_index[0] % levels, branches, token_codes, params, moments, second)


def solution(mesh):
    in_specs = (P(), P("dp", "fsdp"), P("dp", "fsdp", None), P("dp", "fsdp", None), P("dp", "fsdp"))
    out_specs = (P("dp", "fsdp", None), P("dp", "fsdp", None), P("dp", "fsdp"))
    return jax.shard_map(local, mesh=mesh, in_specs=in_specs, out_specs=out_specs, check_vma=False)
```
